32 devices in a mesh: groups: 2 (over y), row: 4 (over x, core), col: 4 (over z).
Axes of the slice: x: 2, y: 2, z: 4, core: 2. Of those that a mesh axis runs over, the one named last changes fastest.
Arguments:
- tile_bits: int32 [8, 4, 96, 32, 256], P(('groups', 'row'), 'col'), parts along dimension 0, may hold values from 0 to 255
- tile_rows: int32 [8, 4, 96], P(('groups', 'row'), 'col'), parts along dimension 0, may hold values from 0 to 3
- tile_cols: int32 [8, 4, 96], P(('groups', 'row'), 'col'), parts along dimension 0, may hold values from 0 to 3
- tile_count: int32 [8, 4], P(('groups', 'row'), 'col'), parts along dimension 0, may hold values from 12 to 96, as said below
- host_order: int32 [8192], P('groups'), parts along dimension 0, may hold values from 0 to 4095, each once
- seed_hosts: int32 [256, 256], P('groups'), parts along dimension 0, may hold values from 0 to 4095
- dangling: int32 [8192], P(('groups', 'col')), parts along dimension 0, may hold values 0 or 1
Outputs:
- rank: float32 [8192, 128], P(('groups', 'row', 'col')), parts along dimension 0
- change: float32 [256], P('groups'), parts along dimension 0
The draws below stay inside these ranges and needn't reach their ends.
There are 2 independent parts, one for each index of `groups`. The reference program is written for one: setup_inputs(seed, part) draws one part's arguments, and reference() takes and returns one part's arrays. A program takes and returns all parts, laid end to end along the dimension named above; each array names one. Nothing has to cross between parts.
Inputs may be any that keep to these rules, and one draw needn't show every extreme that they name: `tile_count`: slots at or past a cell's count hold data that is not part of the graph. Some cell has exactly 96 live slots. `tile_rows`: slots of one cell may name the same block pair; their tiles add.
All inputs are finite; a program needn't handle non-finite values. No bound on the sum of `dangling` on one device may be relied on, other than what follows from the above.
Results may differ from the reference program's by a relative error of at most 0.002.
Values may be sent and summed in bfloat16 or wider, within the bound.
A program may use at most 64 MiB of HBM per device.

```python
import jax
import jax.numpy as jnp
from jax import lax

BS = 256
TOPICS = 128
SEEDS = 256
ITERS = 2
TILE_MAX = 96
NBLK = 4
HOSTS = 4096
N_ROW = 4
N_COL = 4


def draw_tile_count(key, part):
    key = jax.random.fold_in(key, 11)
    key_levels, key_busiest = jax.random.split(key)
    levels = jax.random.randint(key_levels, (N_ROW * N_COL,), 0, 4).astype(jnp.int32)
    counts = jnp.right_shift(jnp.full((N_ROW * N_COL,), TILE_MAX, jnp.int32), levels)
    busiest = jax.random.randint(key_busiest, (), 0, N_ROW * N_COL)
    counts = counts.at[busiest].set(TILE_MAX)
    return counts.reshape(N_ROW, N_COL)


def draw_tile_bits(key, part):
    key = jax.random.fold_in(key, 23)
    key_level, key_dense = jax.random.split(key)
    tile_shape = (N_ROW, N_COL, TILE_MAX, 1, 1)
    levels = jax.random.randint(key_level, tile_shape, 3, 9).astype(jnp.int32)
    dense_pick = jax.random.randint(key_dense, tile_shape, 0, 6) == 0
    levels = jnp.where(dense_pick, 2, levels)
    threshold = jnp.right_shift(jnp.full(tile_shape, 4096, jnp.int32), levels)
    word_shape = (N_ROW, N_COL, TILE_MAX, BS // 8, BS)
    packed_words = jnp.zeros(word_shape, jnp.int32)
    for bit_index in range(8):
        draws = jax.random.randint(jax.random.fold_in(key, 100 + bit_index), word_shape, 0, 4096)
        packed_words = packed_words + jnp.left_shift((draws < threshold).astype(jnp.int32), bit_index)
    return packed_words


def with_ends(array, own_key, smallest, top_value):
    extent = array.shape
    place = [jax.random.randint(jax.random.fold_in(own_key, axis), (), 0, extent[axis]) for axis in range(len(extent))]
    array = array.at[tuple(place)].set(smallest)
    longest = extent.index(max(extent))
    place[longest] = (place[longest] + 1) % extent[longest]
    return array.at[tuple(place)].set(top_value)


def setup_inputs(seed: int = 0, part: int = 0) -> dict:
    arg_keys = jax.random.split(jax.random.key(seed), 8)
    part_splits = jax.random.split(jax.random.fold_in(arg_keys[7], part), 8)
    tile_bits = draw_tile_bits(jax.random.fold_in(jax.random.fold_in(arg_keys[7], part), 71), part)
    tile_rows = with_ends(jax.random.randint(part_splits[1], (N_ROW, N_COL, TILE_MAX), 0, NBLK), jax.random.fold_in(part_splits[1], 1), 0, NBLK - 1).astype(jnp.int32)
    tile_cols = with_ends(jax.random.randint(part_splits[2], (N_ROW, N_COL, TILE_MAX), 0, NBLK), jax.random.fold_in(part_splits[2], 1), 0, NBLK - 1).astype(jnp.int32)
    tile_count = draw_tile_count(jax.random.fold_in(jax.random.fold_in(arg_keys[7], part), 71), part)
    host_order = jax.random.permutation(part_splits[4], HOSTS).astype(jnp.int32)
    seed_hosts = with_ends(jax.random.randint(part_splits[5], (TOPICS, SEEDS), 0, HOSTS), jax.random.fold_in(part_splits[5], 1), 0, HOSTS - 1).astype(jnp.int32)
    dangling = with_ends((jax.random.randint(part_splits[6], (HOSTS,), 0, 4) < 1).astype(jnp.int32), jax.random.fold_in(part_splits[6], 1), 0, 1)
    return {"tile_bits": tile_bits, "tile_rows": tile_rows, "tile_cols": tile_cols, "tile_count": tile_count, "host_order": host_order, "seed_hosts": seed_hosts, "dangling": dangling}


slot_group = 8


def unpack(packed_words):
    bit_shift = jnp.arange(8, dtype=jnp.int32)
    bit_values = jnp.right_shift(packed_words[..., :, None, :], bit_shift[:, None]) & 1
    shape = packed_words.shape
    return bit_values.reshape(shape[:-2] + (shape[-2] * 8, shape[-1]))


def cell_tiles(packed, live_count, first_slot):
    packed_words = lax.dynamic_slice_in_dim(packed, first_slot, slot_group, 0)
    live_slots = (first_slot + jnp.arange(slot_group, dtype=jnp.int32)) < live_count
    return unpack(packed_words).astype(jnp.float32) * live_slots.astype(jnp.float32)[:, None, None]


def reference(tile_bits, tile_rows, tile_cols, tile_count, host_order, seed_hosts, dangling):
    host_total = host_order.shape[0]
    range_hosts = host_total // N_ROW
    block_size = tile_bits.shape[4]
    range_blocks = range_hosts // block_size
    topics = seed_hosts.shape[0]
    cell_total = N_ROW * N_COL
    slot_total = tile_bits.shape[2]
    group_total = slot_total // slot_group
    flat_bits = tile_bits.reshape((cell_total, slot_total) + tile_bits.shape[3:])
    flat_rows = tile_rows.reshape(cell_total, slot_total)
    flat_cols = tile_cols.reshape(cell_total, slot_total)
    flat_count = tile_count.reshape(cell_total)

    def degree_cell(cell_index, running):
        cell_col = cell_index % N_COL

        def group_step(group, inner):
            first_slot = group * slot_group
            dense_tiles = cell_tiles(flat_bits[cell_index], flat_count[cell_index], first_slot)
            group_cols = lax.dynamic_slice_in_dim(flat_cols[cell_index], first_slot, slot_group, 0)
            return inner.at[cell_col, group_cols].add(jnp.sum(dense_tiles, axis=1))

        return lax.fori_loop(0, group_total, group_step, running)

    degree = lax.fori_loop(0, cell_total, degree_cell,
                           jnp.zeros((N_COL, range_blocks, block_size), jnp.float32)).reshape(host_total)
    weight = (1.0 - dangling.astype(jnp.float32)) / jnp.maximum(degree, 1.0)

    positions = host_order[seed_hosts]
    topic_ids = jnp.broadcast_to(jnp.arange(topics, dtype=jnp.int32)[:, None], positions.shape)
    seed_scale = host_total / (16.0 * seed_hosts.shape[1])
    teleport = jnp.zeros((host_total, topics), jnp.float32).at[positions, topic_ids].add(seed_scale)

    def flow_of(scaled_blocks):
        def flow_cell(cell_index, running):
            cell_row = cell_index // N_COL
            cell_col = cell_index % N_COL

            def group_step(group, inner):
                first_slot = group * slot_group
                dense_tiles = cell_tiles(flat_bits[cell_index], flat_count[cell_index], first_slot)
                group_cols = lax.dynamic_slice_in_dim(flat_cols[cell_index], first_slot, slot_group, 0)
                group_rows = lax.dynamic_slice_in_dim(flat_rows[cell_index], first_slot, slot_group, 0)
                sources = scaled_blocks[cell_col][group_cols].astype(jnp.float32)
                product = jnp.einsum("gij,gjk->gik", dense_tiles, sources, precision=lax.Precision.HIGHEST)
                return inner.at[cell_row, group_rows].add(product)

            return lax.fori_loop(0, group_total, group_step, running)

        start = jnp.zeros((N_ROW, range_blocks, block_size, topics), jnp.float32)
        return lax.fori_loop(0, cell_total, flow_cell, start).reshape(host_total, topics)

    rank = teleport
    change = jnp.zeros((topics,), jnp.float32)
    for iteration in range(ITERS):
        source = rank.astype(jnp.bfloat16)
        scaled = (source.astype(jnp.float32) * weight[:, None]).astype(jnp.bfloat16)
        flow = flow_of(scaled.reshape(N_COL, range_blocks, block_size, topics))
        lost_share = jnp.sum(rank, axis=0) - jnp.sum(flow, axis=0)
        new_rank = 0.85 * flow + (0.85 * lost_share / (host_total / 16.0) + 0.15) * teleport
        if iteration == ITERS - 1:
            change = jnp.sum(jnp.abs(new_rank - rank), axis=0) / host_total
        rank = new_rank
    return rank, change
```

```python
import functools

import jax
import jax.numpy as jnp
from jax import lax
from jax.experimental import pallas as pl
from jax.experimental.pallas import tpu as pltpu
from jax.sharding import PartitionSpec as P

LANES = 128
MESH = pl.DeviceIdType.MESH


def cell_kernel(
    sizes, rows_ref, cols_ref, count_ref, bits_hbm, order_ref, seeds_ref,
    a_ref, deg_ref, src_ref, own_ref, bits, acc, dacc, pos, hist, sem,
):
    range_hosts, piece, block, blocks, seed_scale = sizes
    words = block // 8
    topics, seeds = seeds_ref.shape
    row_index = lax.axis_index("row")
    col_index = lax.axis_index("col")
    fetch = pltpu.make_async_copy(bits_hbm, bits, sem)
    fetch.start()
    acc[...] = jnp.zeros_like(acc)
    dacc[...] = jnp.zeros_like(dacc)

    table_rows = order_ref.shape[0]
    parts = seeds // LANES

    def place(group, carry):
        rows8 = pl.ds(pl.multiple_of(group * 8, 8), 8)
        ids = [seeds_ref[rows8, h * LANES:(h + 1) * LANES] for h in range(parts)]
        low = [x & (LANES - 1) for x in ids]
        high = [x >> 7 for x in ids]

        def look(t, found):
            row = jnp.broadcast_to(order_ref[pl.ds(t, 1), :], (8, LANES))
            return tuple(
                jnp.where(high[h] == t,
                          jnp.take_along_axis(row, low[h], axis=1, mode="promise_in_bounds"),
                          found[h])
                for h in range(parts)
            )

        found = lax.fori_loop(0, table_rows, look,
                              tuple(jnp.zeros((8, LANES), jnp.int32) for _ in range(parts)),
                              unroll=8)
        for h in range(parts):
            pos[rows8, h * LANES:(h + 1) * LANES] = found[h]
        return carry

    lax.fori_loop(0, topics // 8, place, 0)

    src_high = range_hosts // LANES
    own_high = piece // LANES
    high_rows = hist.shape[0] // topics
    t = lax.broadcasted_iota(jnp.int32, (high_rows, seeds), 0)
    first_src = col_index * src_high
    first_own = row_index * src_high + col_index * own_high
    wanted = jnp.where(t < src_high, first_src + t,
                       jnp.where(t < src_high + own_high, first_own + t - src_high, -1))
    lane_id = lax.broadcasted_iota(jnp.int32, (LANES, seeds), 0)

    def count(k, carry):
        row = pos[pl.ds(k, 1), :]
        low = jnp.where((row & (LANES - 1)) == lane_id, 1.0, 0.0).astype(jnp.bfloat16)
        high = jnp.where((row >> 7) == wanted, 1.0, 0.0).astype(jnp.bfloat16)
        hist[pl.ds(pl.multiple_of(k * high_rows, 8), high_rows), :] = lax.dot_general(
            high, low, (((1,), (1,)), ((), ())), preferred_element_type=jnp.float32)
        return carry

    lax.fori_loop(0, topics, count, 0, unroll=8)
    for i in range(src_high):
        src_ref[i * LANES:(i + 1) * LANES, :] = (
            hist[pl.ds(i, topics, stride=high_rows), :].T * seed_scale)
    for i in range(own_high):
        own_ref[i * LANES:(i + 1) * LANES, :] = (
            hist[pl.ds(src_high + i, topics, stride=high_rows), :].T * seed_scale)

    fetch.wait()

    def add_tile(s, carry):
        pair = rows_ref[s] * blocks + cols_ref[s]
        w = bits[s]
        w = w | (w << 7)
        w = w | (w << 14)
        acc[pair, 0] = acc[pair, 0] + (w & 0x01010101)
        acc[pair, 1] = acc[pair, 1] + ((w >> 4) & 0x01010101)
        return carry

    lax.fori_loop(0, count_ref[0], add_tile, 0)

    def expand(pair, carry):
        first_row = (pair // blocks) * block
        col = pair % blocks
        cols = pl.ds(pl.multiple_of(col * block, block), block)
        total = dacc[col]
        for half in range(2):
            packed = acc[pair, half]
            for b in range(4):
                v = (packed >> (8 * b)) & 255
                total = total + v
                start = pl.multiple_of(first_row + (half * 4 + b) * words, 16)
                a_ref[pl.ds(start, words), cols] = v.astype(jnp.float32).astype(jnp.bfloat16)
        dacc[col] = total
        return carry

    lax.fori_loop(0, blocks * blocks, expand, 0)
    per = block // LANES
    for col in range(blocks):
        sums = jnp.sum(dacc[col], axis=0, keepdims=True).astype(jnp.float32)
        for i in range(per):
            deg_ref[col * per + i:col * per + i + 1, :] = sums[:, i * LANES:(i + 1) * LANES]


def rank_kernel(
    sizes, a_ref, deg_ref, dang_ref, src_ref, own_ref, rank_ref, change_ref,
    degs, wrow, drow, wcol, dcol, scaled, nat, own_flow, sbuf1, sbuf2, recv_b, recv_c, recv_t,
    rank1, recv_d, lost1, lost2, chg,
    deg_s, deg_r, l1_s, l1_r, l2_s, l2_r, b_s, b_r, c_s, c_r, t_s, t_r, d_s, d_r, e_s, e_r,
):
    n_row, n_col, range_hosts, piece, block, host_total = sizes
    words = block // 8
    r = lax.axis_index("row")
    c = lax.axis_index("col")
    me = r * n_col + c
    total_mass = host_total / 16.0
    chunks = range_hosts // LANES

    def each(n, body):
        lax.fori_loop(0, n, lambda i, carry: (body(i), carry)[1], 0)

    def others(n, mine, body):
        def step(i):
            @pl.when(i != mine)
            def _():
                body(i)
        each(n, step)

    def remote(src, dst, send, recv, row, col):
        return pltpu.make_async_remote_copy(
            src_ref=src, dst_ref=dst, send_sem=send, recv_sem=recv,
            device_id={"row": row, "col": col}, device_id_type=MESH)

    barrier = pltpu.get_barrier_semaphore()
    others(n_row * n_col, me, lambda i: pl.semaphore_signal(
        barrier, inc=1, device_id={"row": i // n_col, "col": i % n_col}, device_id_type=MESH))
    pl.semaphore_wait(barrier, n_row * n_col - 1)

    def deg_copy(i, slot):
        return remote(deg_ref, degs.at[slot], deg_s.at[i], deg_r.at[slot], i, c)

    others(n_row, r, lambda i: deg_copy(i, r).start())
    degs[r] = deg_ref[...]
    others(n_row, r, lambda i: deg_copy(i, i).wait_recv())
    degree = degs[0]
    for i in range(1, n_row):
        degree = degree + degs[i]
    wrow[...] = (1.0 - dang_ref[...].astype(jnp.float32)) / jnp.maximum(degree, 1.0)
    drow[...] = degree

    def spread(i):
        rows = pl.ds(pl.multiple_of(i * LANES, LANES), LANES)
        wcol[rows, :] = jnp.broadcast_to(wrow[pl.ds(i, 1), :], (LANES, LANES)).T
        dcol[rows, :] = jnp.broadcast_to(drow[pl.ds(i, 1), :], (LANES, LANES)).T

    each(chunks, spread)

    def make_scaled(source_of, lost, send, recv):
        def step(i, total):
            rows = pl.ds(pl.multiple_of(i * LANES, LANES), LANES)
            part = (source_of(i, rows).astype(jnp.float32) * wcol[rows, :]).astype(jnp.bfloat16)
            scaled[rows, :] = part
            mass = dcol[rows, :] * part.astype(jnp.float32)
            return total + jnp.sum(mass.reshape(LANES // 8, 8, LANES), axis=0)

        lost[c] = lax.fori_loop(0, chunks, step, jnp.zeros((8, LANES), jnp.float32))
        others(n_col, c, lambda i: lost_copy(lost, send, recv, i, c).start())

    def lost_copy(lost, send, recv, i, slot):
        return remote(lost.at[c], lost.at[slot], send.at[i], recv.at[slot], r, i)

    def coefficient(lost, send, recv):
        others(n_col, c, lambda i: lost_copy(lost, send, recv, i, i).wait_recv())
        total = lost[0]
        for i in range(1, n_col):
            total = total + lost[i]
        gone = total_mass - jnp.sum(total, axis=0, keepdims=True)
        return 0.85 * gone / total_mass + 0.15

    def flow_piece(q, sbuf):
        for sub in range(piece // block):
            first = pl.multiple_of(q * piece + sub * block, block)
            product = jnp.dot(a_ref[pl.ds(first, block), :], scaled[...],
                              preferred_element_type=jnp.float32)
            for bit in range(8):
                nat[pl.ds(sub * block + bit, words, stride=8), :] = (
                    product[bit * words:(bit + 1) * words, :])
        sbuf[q] = nat[...].astype(jnp.bfloat16)

    make_scaled(lambda i, rows: src_ref[rows, :].astype(jnp.bfloat16), lost1, l1_s, l1_r)
    diagonal = r == c

    def b_copy(q, slot):
        return remote(sbuf1.at[q], recv_b.at[slot], b_s.at[q], b_r.at[slot], q, r)

    def first_piece(i):
        q = lax.rem(r + 1 + i, n_row)
        flow_piece(q, sbuf1)
        home = jnp.logical_and(diagonal, q == r)

        @pl.when(jnp.logical_not(home))
        def _():
            b_copy(q, c).start()

        @pl.when(home)
        def _():
            recv_b[c] = sbuf1[q]

    each(n_row, first_piece)
    share1 = coefficient(lost1, l1_s, l1_r)

    def b_wait(i):
        @pl.when(jnp.logical_not(jnp.logical_and(diagonal, i == c)))
        def _():
            b_copy(0, i).wait_recv()

    each(n_col, b_wait)
    flow = recv_b[0].astype(jnp.float32)
    for i in range(1, n_col):
        flow = flow + recv_b[i].astype(jnp.float32)
    tele = src_ref[pl.ds(pl.multiple_of(r * piece, piece), piece), :]
    new_rank = 0.85 * flow + share1 * tele
    recv_c[r] = new_rank.astype(jnp.bfloat16)

    def c_copy(i, slot):
        return remote(recv_c.at[r], recv_c.at[slot], c_s.at[i], c_r.at[slot], i, c)

    others(n_row, r, lambda i: c_copy(i, r).start())
    rank1[...] = new_rank
    t_copy = remote(rank1, recv_t, t_s, t_r, c, r)

    @pl.when(jnp.logical_not(diagonal))
    def _():
        t_copy.start()

    @pl.when(diagonal)
    def _():
        recv_t[...] = rank1[...]

    others(n_row, r, lambda i: c_copy(i, i).wait_recv())

    per = piece // LANES

    def second_source(i, rows):
        inner = pl.ds(pl.multiple_of((i % per) * LANES, LANES), LANES)
        return recv_c[i // per, inner, :]

    make_scaled(second_source, lost2, l2_s, l2_r)

    def d_copy(q, slot):
        return remote(sbuf2.at[q], recv_d.at[slot], d_s.at[q], d_r.at[slot], r, q)

    def second_piece(i):
        q = lax.rem(c + 1 + i, n_col)
        flow_piece(q, sbuf2)

        @pl.when(q != c)
        def _():
            d_copy(q, c).start()

        @pl.when(q == c)
        def _():
            own_flow[...] = nat[...]

    each(n_col, second_piece)
    share2 = coefficient(lost2, l2_s, l2_r)
    recv_d[c] = jnp.zeros((piece, LANES), jnp.bfloat16)

    @pl.when(jnp.logical_not(diagonal))
    def _():
        t_copy.wait_recv()

    others(n_col, c, lambda i: d_copy(0, i).wait_recv())
    flow = own_flow[...]
    for i in range(n_col):
        flow = flow + recv_d[i].astype(jnp.float32)
    last = 0.85 * flow + share2 * own_ref[...]
    moved = jnp.abs(last - recv_t[...])
    chg[me] = jnp.sum(moved.reshape(piece // 8, 8, LANES), axis=0)

    def e_copy(i, slot):
        return remote(chg.at[me], chg.at[slot], e_s.at[i], e_r.at[slot], i // n_col, i % n_col)

    others(n_row * n_col, me, lambda i: e_copy(i, me).start())
    rank_ref[...] = last
    others(n_row, r, lambda i: deg_copy(i, r).wait_send())
    others(n_col, c, lambda i: lost_copy(lost1, l1_s, l1_r, i, c).wait_send())
    others(n_col, c, lambda i: lost_copy(lost2, l2_s, l2_r, i, c).wait_send())

    def b_sent(q):
        @pl.when(jnp.logical_not(jnp.logical_and(diagonal, q == r)))
        def _():
            b_copy(q, c).wait_send()

    each(n_row, b_sent)
    others(n_row, r, lambda i: c_copy(i, r).wait_send())

    @pl.when(jnp.logical_not(diagonal))
    def _():
        t_copy.wait_send()

    others(n_col, c, lambda i: d_copy(i, c).wait_send())
    others(n_row * n_col, me, lambda i: e_copy(i, i).wait_recv())
    total = lax.fori_loop(0, n_row * n_col, lambda i, x: x + chg[i],
                          jnp.zeros((8, LANES), jnp.float32))
    change_ref[...] = jnp.sum(total, axis=0, keepdims=True) / host_total
    others(n_row * n_col, me, lambda i: e_copy(i, me).wait_send())


def shards(n_row, n_col, tile_bits, tile_rows, tile_cols, tile_count, host_order, seed_hosts,
           dangling):
    packed = tile_bits[0, 0]
    slots, words, block = packed.shape
    host_total = host_order.shape[0]
    range_hosts = dangling.shape[0]
    blocks = range_hosts // block
    topics, seeds = seed_hosts.shape
    piece = range_hosts // n_col
    assert slots < 128 and topics == LANES and n_row == n_col and piece % block == 0
    seed_scale = host_total / (16.0 * seeds)
    f32, bf16, i32 = jnp.float32, jnp.bfloat16, jnp.int32
    chunks = range_hosts // LANES
    high_rows = -(-(range_hosts + piece) // (LANES * 8)) * 8
    vmem = pl.BlockSpec(memory_space=pltpu.VMEM)
    smem = pl.BlockSpec(memory_space=pltpu.SMEM)
    adjacency, degree, tele_src, tele_own = pl.pallas_call(
        functools.partial(cell_kernel, (range_hosts, piece, block, blocks, seed_scale)),
        out_shape=[
            jax.ShapeDtypeStruct((range_hosts, range_hosts), bf16),
            jax.ShapeDtypeStruct((chunks, LANES), f32),
            jax.ShapeDtypeStruct((range_hosts, topics), f32),
            jax.ShapeDtypeStruct((piece, topics), f32),
        ],
        in_specs=[smem, smem, smem, pl.BlockSpec(memory_space=pl.ANY), vmem, vmem],
        out_specs=[vmem] * 4,
        scratch_shapes=[
            pltpu.VMEM((slots, words, block), i32),
            pltpu.VMEM((blocks * blocks, 2, words, block), i32),
            pltpu.VMEM((blocks, words, block), i32),
            pltpu.VMEM((topics, seeds), i32),
            pltpu.VMEM((topics * high_rows, LANES), f32),
            pltpu.SemaphoreType.DMA,
        ],
        compiler_params=pltpu.CompilerParams(vmem_limit_bytes=60 * 2**20),
        name="cell",
    )(tile_rows[0, 0], tile_cols[0, 0], tile_count[0], packed,
      host_order.reshape(host_total // LANES, LANES), seed_hosts)

    devices = n_row * n_col
    dma = lambda n: pltpu.SemaphoreType.DMA((n,))
    rank, change = pl.pallas_call(
        functools.partial(rank_kernel, (n_row, n_col, range_hosts, piece, block, host_total)),
        out_shape=[
            jax.ShapeDtypeStruct((piece, topics), f32),
            jax.ShapeDtypeStruct((1, topics), f32),
        ],
        in_specs=[vmem] * 5,
        out_specs=[vmem] * 2,
        scratch_shapes=[
            pltpu.VMEM((n_row, chunks, LANES), f32),
            pltpu.VMEM((chunks, LANES), f32),
            pltpu.VMEM((chunks, LANES), f32),
            pltpu.VMEM((range_hosts, topics), f32),
            pltpu.VMEM((range_hosts, topics), f32),
            pltpu.VMEM((range_hosts, topics), bf16),
            pltpu.VMEM((piece, topics), f32),
            pltpu.VMEM((piece, topics), f32),
            pltpu.VMEM((n_row, piece, topics), bf16),
            pltpu.VMEM((n_col, piece, topics), bf16),
            pltpu.VMEM((n_col, piece, topics), bf16),
            pltpu.VMEM((n_row, piece, topics), bf16),
            pltpu.VMEM((piece, topics), f32),
            pltpu.VMEM((piece, topics), f32),
            pltpu.VMEM((n_col, piece, topics), bf16),
            pltpu.VMEM((n_col, 8, topics), f32),
            pltpu.VMEM((n_col, 8, topics), f32),
            pltpu.VMEM((devices, 8, topics), f32),
            dma(n_row), dma(n_row),
            dma(n_col), dma(n_col), dma(n_col), dma(n_col),
            dma(n_row), dma(n_col),
            dma(n_row), dma(n_row),
            pltpu.SemaphoreType.DMA, pltpu.SemaphoreType.DMA,
            dma(n_col), dma(n_col),
            dma(devices), dma(devices),
        ],
        compiler_params=pltpu.CompilerParams(
            collective_id=0, has_side_effects=True, vmem_limit_bytes=60 * 2**20),
        name="iterate",
    )(adjacency, degree, dangling.reshape(chunks, LANES), tele_src, tele_own)
    return (rank, change.reshape(topics))


def solution(mesh):
    in_specs = (
        P(("groups", "row"), "col", None, None, None),
        P(("groups", "row"), "col", None),
        P(("groups", "row"), "col", None),
        P(("groups", "row"), "col"),
        P("groups"),
        P("groups", None),
        P(("groups", "col")),
    )
    out_specs = (P(("groups", "row", "col"), None), P("groups"))
    body = functools.partial(shards, mesh.shape["row"], mesh.shape["col"])
    return jax.shard_map(body, mesh=mesh, in_specs=in_specs, out_specs=out_specs, check_vma=False)
```

```python
import functools

import jax
import jax.numpy as jnp
from jax import lax
from jax.experimental import pallas as pl
from jax.experimental.pallas import tpu as pltpu
from jax.sharding import PartitionSpec as P

LANES = 128
MESH = pl.DeviceIdType.MESH


def cell_kernel(
    sizes, rows_ref, cols_ref, count_ref, bits_hbm, a_ref, deg_ref, bits, acc, dacc, sem,
):
    block, blocks = sizes
    words = block // 8
    fetch = pltpu.make_async_copy(bits_hbm, bits, sem)
    fetch.start()
    acc[...] = jnp.zeros_like(acc)
    dacc[...] = jnp.zeros_like(dacc)

    fetch.wait()

    def add_tile(s, carry):
        pair = rows_ref[s] * blocks + cols_ref[s]
        w = bits[s]
        w = w | (w << 7)
        w = w | (w << 14)
        acc[pair, 0] = acc[pair, 0] + (w & 0x01010101)
        acc[pair, 1] = acc[pair, 1] + ((w >> 4) & 0x01010101)
        return carry

    lax.fori_loop(0, count_ref[0], add_tile, 0)

    def expand(pair, carry):
        first_row = (pair // blocks) * block
        col = pair % blocks
        cols = pl.ds(pl.multiple_of(col * block, block), block)
        total = dacc[col]
        for half in range(2):
            packed = acc[pair, half]
            for b in range(4):
                v = (packed >> (8 * b)) & 255
                total = total + v
                start = pl.multiple_of(first_row + (half * 4 + b) * words, 16)
                a_ref[pl.ds(start, words), cols] = v.astype(jnp.float32).astype(jnp.bfloat16)
        dacc[col] = total
        return carry

    lax.fori_loop(0, blocks * blocks, expand, 0)
    per = block // LANES
    for col in range(blocks):
        sums = jnp.sum(dacc[col], axis=0, keepdims=True).astype(jnp.float32)
        for i in range(per):
            deg_ref[col * per + i:col * per + i + 1, :] = sums[:, i * LANES:(i + 1) * LANES]


def rank_kernel(
    sizes, a_hbm, deg_ref, dang_ref, order_ref, seeds_ref, rank_ref, change_ref,
    a_ref, pos, hist, hist_bf, src_ref, tele_bf, own_bf,
    degs, wcol, dcol, scaled, nat, own_flow, sbuf1, sbuf2, recv_b, recv_c, recv_t,
    rank1, recv_d, lost1, lost2, chg, a_sem,
    deg_s, deg_r, h_s, h_r, o_s, o_r, l1_s, l1_r, l2_s, l2_r, b_s, b_r, c_s, c_r, t_s, t_r,
    d_s, d_r, e_s, e_r,
):
    n_row, n_col, range_hosts, piece, block, host_total, seed_scale = sizes
    words = block // 8
    r = lax.axis_index("row")
    c = lax.axis_index("col")
    me = r * n_col + c
    total_mass = host_total / 16.0
    chunks = range_hosts // LANES

    def each(n, body):
        lax.fori_loop(0, n, lambda i, carry: (body(i), carry)[1], 0)

    def others(n, mine, body):
        def step(i):
            @pl.when(i != mine)
            def _():
                body(i)
        each(n, step)

    def remote(src, dst, send, recv, row, col):
        return pltpu.make_async_remote_copy(
            src_ref=src, dst_ref=dst, send_sem=send, recv_sem=recv,
            device_id={"row": row, "col": col}, device_id_type=MESH)

    barrier = pltpu.get_barrier_semaphore()
    others(n_row * n_col, me, lambda i: pl.semaphore_signal(
        barrier, inc=1, device_id={"row": i // n_col, "col": i % n_col}, device_id_type=MESH))

    fetch = pltpu.make_async_copy(a_hbm, a_ref, a_sem)
    fetch.start()
    topics, seeds = seeds_ref.shape
    share = topics // n_row
    table_rows = order_ref.shape[0]
    parts = seeds // LANES

    def place(group, carry):
        rows8 = pl.ds(pl.multiple_of(r * share + group * 8, 8), 8)
        ids = [seeds_ref[rows8, h * LANES:(h + 1) * LANES] for h in range(parts)]
        low = [x & (LANES - 1) for x in ids]
        high = [x >> 7 for x in ids]

        def look(t, found):
            row = jnp.broadcast_to(order_ref[pl.ds(t, 1), :], (8, LANES))
            return tuple(
                jnp.where(high[h] == t,
                          jnp.take_along_axis(row, low[h], axis=1, mode="promise_in_bounds"),
                          found[h])
                for h in range(parts)
            )

        found = lax.fori_loop(0, table_rows, look,
                              tuple(jnp.zeros((8, LANES), jnp.int32) for _ in range(parts)),
                              unroll=8)
        for h in range(parts):
            pos[pl.ds(pl.multiple_of(group * 8, 8), 8), h * LANES:(h + 1) * LANES] = found[h]
        return carry

    lax.fori_loop(0, share // 8, place, 0)
    wanted = c * chunks + lax.broadcasted_iota(jnp.int32, (chunks, seeds), 0)
    lane_id = lax.broadcasted_iota(jnp.int32, (LANES, seeds), 0)

    def count(k, carry):
        row = pos[pl.ds(k, 1), :]
        low = jnp.where((row & (LANES - 1)) == lane_id, 1.0, 0.0).astype(jnp.bfloat16)
        high = jnp.where((row >> 7) == wanted, 1.0, 0.0).astype(jnp.bfloat16)
        hist[pl.ds(pl.multiple_of(k * chunks, 8), chunks), :] = lax.dot_general(
            high, low, (((1,), (1,)), ((), ())), preferred_element_type=jnp.float32)
        return carry

    lax.fori_loop(0, share, count, 0, unroll=8)
    hist_bf[r] = hist[pl.ds(0, share * chunks), :].astype(jnp.bfloat16)
    pl.semaphore_wait(barrier, n_row * n_col - 1)

    def deg_copy(i, slot):
        return remote(deg_ref, degs.at[slot], deg_s.at[i], deg_r.at[slot], i, c)

    def hist_copy(i, slot):
        return remote(hist_bf.at[r], hist_bf.at[slot], h_s.at[i], h_r.at[slot], i, c)

    others(n_row, r, lambda i: deg_copy(i, r).start())
    others(n_row, r, lambda i: hist_copy(i, r).start())
    degs[r] = deg_ref[...]
    others(n_row, r, lambda i: deg_copy(i, i).wait_recv())
    degree = degs[0]
    for i in range(1, n_row):
        degree = degree + degs[i]
    weight = ((1.0 - dang_ref[...].astype(jnp.float32)) / jnp.maximum(degree, 1.0)).T
    degree = degree.T
    for i in range(chunks):
        rows = slice(i * LANES, (i + 1) * LANES)
        wcol[rows, :] = jnp.broadcast_to(weight[:, i:i + 1], (LANES, LANES))
        dcol[rows, :] = jnp.broadcast_to(degree[:, i:i + 1], (LANES, LANES))

    others(n_row, r, lambda i: hist_copy(i, i).wait_recv())
    slab = share * chunks
    for i in range(n_row):
        hist[i * slab:(i + 1) * slab, :] = hist_bf[i].astype(jnp.float32)
    for i in range(chunks):
        tele_bf[i * LANES:(i + 1) * LANES, :] = (
            hist[pl.ds(i, topics, stride=chunks), :].T.astype(jnp.bfloat16))
    src_ref[...] = tele_bf[...].astype(jnp.float32) * seed_scale
    diagonal = r == c
    quarter = pl.ds(pl.multiple_of(r * piece, piece), piece)
    o_copy = remote(tele_bf.at[quarter], own_bf, o_s, o_r, c, r)

    @pl.when(jnp.logical_not(diagonal))
    def _():
        o_copy.start()

    @pl.when(diagonal)
    def _():
        own_bf[...] = tele_bf[quarter, :]

    def make_scaled(source_of, lost, send, recv):
        def step(i, total):
            rows = pl.ds(pl.multiple_of(i * LANES, LANES), LANES)
            part = (source_of(i, rows).astype(jnp.float32) * wcol[rows, :]).astype(jnp.bfloat16)
            scaled[rows, :] = part
            mass = dcol[rows, :] * part.astype(jnp.float32)
            return total + jnp.sum(mass.reshape(LANES // 8, 8, LANES), axis=0)

        lost[c] = lax.fori_loop(0, chunks, step, jnp.zeros((8, LANES), jnp.float32))
        others(n_col, c, lambda i: lost_copy(lost, send, recv, i, c).start())

    def lost_copy(lost, send, recv, i, slot):
        return remote(lost.at[c], lost.at[slot], send.at[i], recv.at[slot], r, i)

    def coefficient(lost, send, recv):
        others(n_col, c, lambda i: lost_copy(lost, send, recv, i, i).wait_recv())
        total = lost[0]
        for i in range(1, n_col):
            total = total + lost[i]
        gone = total_mass - jnp.sum(total, axis=0, keepdims=True)
        return 0.85 * gone / total_mass + 0.15

    def flow_piece(q, sbuf):
        for sub in range(piece // block):
            first = pl.multiple_of(q * piece + sub * block, block)
            product = jnp.dot(a_ref[pl.ds(first, block), :], scaled[...],
                              preferred_element_type=jnp.float32)
            for bit in range(8):
                nat[pl.ds(sub * block + bit, words, stride=8), :] = (
                    product[bit * words:(bit + 1) * words, :])
        sbuf[q] = nat[...].astype(jnp.bfloat16)

    make_scaled(lambda i, rows: src_ref[rows, :].astype(jnp.bfloat16), lost1, l1_s, l1_r)
    fetch.wait()

    def b_copy(q, slot):
        return remote(sbuf1.at[q], recv_b.at[slot], b_s.at[q], b_r.at[slot], q, r)

    def first_piece(i):
        q = lax.rem(r + 1 + i, n_row)
        flow_piece(q, sbuf1)
        home = jnp.logical_and(diagonal, q == r)

        @pl.when(jnp.logical_not(home))
        def _():
            b_copy(q, c).start()

        @pl.when(home)
        def _():
            recv_b[c] = sbuf1[q]

    each(n_row, first_piece)
    share1 = coefficient(lost1, l1_s, l1_r)

    def b_wait(i):
        @pl.when(jnp.logical_not(jnp.logical_and(diagonal, i == c)))
        def _():
            b_copy(0, i).wait_recv()

    each(n_col, b_wait)
    flow = recv_b[0].astype(jnp.float32)
    for i in range(1, n_col):
        flow = flow + recv_b[i].astype(jnp.float32)
    tele = src_ref[quarter, :]
    new_rank = 0.85 * flow + share1 * tele
    recv_c[r] = new_rank.astype(jnp.bfloat16)

    def c_copy(i, slot):
        return remote(recv_c.at[r], recv_c.at[slot], c_s.at[i], c_r.at[slot], i, c)

    others(n_row, r, lambda i: c_copy(i, r).start())
    rank1[...] = new_rank
    t_copy = remote(rank1, recv_t, t_s, t_r, c, r)

    @pl.when(jnp.logical_not(diagonal))
    def _():
        t_copy.start()

    @pl.when(diagonal)
    def _():
        recv_t[...] = rank1[...]

    others(n_row, r, lambda i: c_copy(i, i).wait_recv())

    per = piece // LANES

    def second_source(i, rows):
        inner = pl.ds(pl.multiple_of((i % per) * LANES, LANES), LANES)
        return recv_c[i // per, inner, :]

    make_scaled(second_source, lost2, l2_s, l2_r)

    def d_copy(q, slot):
        return remote(sbuf2.at[q], recv_d.at[slot], d_s.at[q], d_r.at[slot], r, q)

    def second_piece(i):
        q = lax.rem(c + 1 + i, n_col)
        flow_piece(q, sbuf2)

        @pl.when(q != c)
        def _():
            d_copy(q, c).start()

        @pl.when(q == c)
        def _():
            own_flow[...] = nat[...]

    each(n_col, second_piece)
    share2 = coefficient(lost2, l2_s, l2_r)
    recv_d[c] = jnp.zeros((piece, LANES), jnp.bfloat16)

    @pl.when(jnp.logical_not(diagonal))
    def _():
        t_copy.wait_recv()
        o_copy.wait_recv()

    others(n_col, c, lambda i: d_copy(0, i).wait_recv())
    flow = own_flow[...]
    for i in range(n_col):
        flow = flow + recv_d[i].astype(jnp.float32)
    last = 0.85 * flow + share2 * (own_bf[...].astype(jnp.float32) * seed_scale)
    moved = jnp.abs(last - recv_t[...])
    chg[me] = jnp.sum(moved.reshape(piece // 8, 8, LANES), axis=0)

    def e_copy(i, slot):
        return remote(chg.at[me], chg.at[slot], e_s.at[i], e_r.at[slot], i // n_col, i % n_col)

    others(n_row * n_col, me, lambda i: e_copy(i, me).start())
    rank_ref[...] = last
    others(n_row, r, lambda i: deg_copy(i, r).wait_send())
    others(n_row, r, lambda i: hist_copy(i, r).wait_send())
    others(n_col, c, lambda i: lost_copy(lost1, l1_s, l1_r, i, c).wait_send())
    others(n_col, c, lambda i: lost_copy(lost2, l2_s, l2_r, i, c).wait_send())

    def b_sent(q):
        @pl.when(jnp.logical_not(jnp.logical_and(diagonal, q == r)))
        def _():
            b_copy(q, c).wait_send()

    each(n_row, b_sent)
    others(n_row, r, lambda i: c_copy(i, r).wait_send())

    @pl.when(jnp.logical_not(diagonal))
    def _():
        t_copy.wait_send()
        o_copy.wait_send()

    others(n_col, c, lambda i: d_copy(i, c).wait_send())
    others(n_row * n_col, me, lambda i: e_copy(i, i).wait_recv())
    total = lax.fori_loop(0, n_row * n_col, lambda i, x: x + chg[i],
                          jnp.zeros((8, LANES), jnp.float32))
    change_ref[...] = total
    others(n_row * n_col, me, lambda i: e_copy(i, me).wait_send())


def give_kernel(host_total, last_ref, moved_ref, rank_ref, change_ref):
    rank_ref[...] = last_ref[...]
    change_ref[...] = jnp.sum(moved_ref[...], axis=0, keepdims=True) / host_total


def shards(n_row, n_col, tile_bits, tile_rows, tile_cols, tile_count, host_order, seed_hosts,
           dangling):
    packed = tile_bits[0, 0]
    slots, words, block = packed.shape
    host_total = host_order.shape[0]
    range_hosts = dangling.shape[0]
    blocks = range_hosts // block
    topics, seeds = seed_hosts.shape
    piece = range_hosts // n_col
    assert slots < 128 and topics == LANES and n_row == n_col and piece % block == 0
    assert seeds <= 256 and topics % (8 * n_row) == 0
    seed_scale = host_total / (16.0 * seeds)
    f32, bf16, i32 = jnp.float32, jnp.bfloat16, jnp.int32
    chunks = range_hosts // LANES
    vmem = pl.BlockSpec(memory_space=pltpu.VMEM)
    smem = pl.BlockSpec(memory_space=pltpu.SMEM)
    hbm = pl.BlockSpec(memory_space=pl.ANY)
    adjacency, degree = pl.pallas_call(
        functools.partial(cell_kernel, (block, blocks)),
        out_shape=[
            jax.ShapeDtypeStruct((range_hosts, range_hosts), bf16),
            jax.ShapeDtypeStruct((chunks, LANES), f32),
        ],
        in_specs=[smem, smem, smem, hbm],
        out_specs=[vmem] * 2,
        scratch_shapes=[
            pltpu.VMEM((slots, words, block), i32),
            pltpu.VMEM((blocks * blocks, 2, words, block), i32),
            pltpu.VMEM((blocks, words, block), i32),
            pltpu.SemaphoreType.DMA,
        ],
        compiler_params=pltpu.CompilerParams(vmem_limit_bytes=60 * 2**20),
        name="cell",
    )(tile_rows[0, 0], tile_cols[0, 0], tile_count[0], packed)

    devices = n_row * n_col
    dma = lambda n: pltpu.SemaphoreType.DMA((n,))
    last, moved = pl.pallas_call(
        functools.partial(rank_kernel, (n_row, n_col, range_hosts, piece, block, host_total,
                                        seed_scale)),
        out_shape=[
            jax.ShapeDtypeStruct((piece, topics), f32),
            jax.ShapeDtypeStruct((8, topics), f32),
        ],
        in_specs=[hbm] + [vmem] * 4,
        out_specs=[vmem] * 2,
        scratch_shapes=[
            pltpu.VMEM((range_hosts, range_hosts), bf16),
            pltpu.VMEM((topics // n_row, seeds), i32),
            pltpu.VMEM((topics * chunks, LANES), f32),
            pltpu.VMEM((n_row, topics // n_row * chunks, LANES), bf16),
            pltpu.VMEM((range_hosts, topics), f32),
            pltpu.VMEM((range_hosts, topics), bf16),
            pltpu.VMEM((piece, topics), bf16),
            pltpu.VMEM((n_row, chunks, LANES), f32),
            pltpu.VMEM((range_hosts, topics), f32),
            pltpu.VMEM((range_hosts, topics), f32),
            pltpu.VMEM((range_hosts, topics), bf16),
            pltpu.VMEM((piece, topics), f32),
            pltpu.VMEM((piece, topics), f32),
            pltpu.VMEM((n_row, piece, topics), bf16),
            pltpu.VMEM((n_col, piece, topics), bf16),
            pltpu.VMEM((n_col, piece, topics), bf16),
            pltpu.VMEM((n_row, piece, topics), bf16),
            pltpu.VMEM((piece, topics), f32),
            pltpu.VMEM((piece, topics), f32),
            pltpu.VMEM((n_col, piece, topics), bf16),
            pltpu.VMEM((n_col, 8, topics), f32),
            pltpu.VMEM((n_col, 8, topics), f32),
            pltpu.VMEM((devices, 8, topics), f32),
            pltpu.SemaphoreType.DMA,
            dma(n_row), dma(n_row), dma(n_row), dma(n_row),
            pltpu.SemaphoreType.DMA, pltpu.SemaphoreType.DMA,
            dma(n_col), dma(n_col), dma(n_col), dma(n_col),
            dma(n_row), dma(n_col),
            dma(n_row), dma(n_row),
            pltpu.SemaphoreType.DMA, pltpu.SemaphoreType.DMA,
            dma(n_col), dma(n_col),
            dma(devices), dma(devices),
        ],
        compiler_params=pltpu.CompilerParams(
            collective_id=0, has_side_effects=True, vmem_limit_bytes=60 * 2**20),
        name="iterate",
    )(adjacency, degree, dangling.reshape(chunks, LANES),
      host_order.reshape(host_total // LANES, LANES), seed_hosts)
    rank, change = pl.pallas_call(
        functools.partial(give_kernel, host_total),
        out_shape=[
            jax.ShapeDtypeStruct((piece, topics), f32),
            jax.ShapeDtypeStruct((1, topics), f32),
        ],
        in_specs=[vmem] * 2,
        out_specs=[vmem] * 2,
        name="give",
    )(last, moved)
    return (rank, change.reshape(topics))


def solution(mesh):
    in_specs = (
        P(("groups", "row"), "col", None, None, None),
        P(("groups", "row"), "col", None),
        P(("groups", "row"), "col", None),
        P(("groups", "row"), "col"),
        P("groups"),
        P("groups", None),
        P(("groups", "col")),
    )
    out_specs = (P(("groups", "row", "col"), None), P("groups"))
    body = functools.partial(shards, mesh.shape["row"], mesh.shape["col"])
    return jax.shard_map(body, mesh=mesh, in_specs=in_specs, out_specs=out_specs, check_vma=False)
```

```python
import functools

import jax
import jax.numpy as jnp
from jax import lax
from jax.experimental import pallas as pl
from jax.experimental.pallas import tpu as pltpu
from jax.sharding import PartitionSpec as P

LANES = 128
MESH = pl.DeviceIdType.MESH


def cell_kernel(
    sizes, rows_ref, cols_ref, count_ref, bits_hbm, a_ref, deg_ref, bits, acc, dacc, sem,
):
    block, blocks = sizes
    words = block // 8
    fetch = pltpu.make_async_copy(bits_hbm, bits, sem)
    fetch.start()
    acc[...] = jnp.zeros_like(acc)
    dacc[...] = jnp.zeros_like(dacc)

    fetch.wait()

    def add_tile(s, carry):
        pair = rows_ref[s] * blocks + cols_ref[s]
        w = bits[s]
        w = w | (w << 7)
        w = w | (w << 14)
        acc[pair, 0] = acc[pair, 0] + (w & 0x01010101)
        acc[pair, 1] = acc[pair, 1] + ((w >> 4) & 0x01010101)
        return carry

    lax.fori_loop(0, count_ref[0], add_tile, 0)

    def expand(pair, carry):
        first_row = (pair // blocks) * block
        col = pair % blocks
        cols = pl.ds(pl.multiple_of(col * block, block), block)
        total = dacc[col]
        for half in range(2):
            packed = acc[pair, half]
            for b in range(4):
                v = (packed >> (8 * b)) & 255
                total = total + v
                start = pl.multiple_of(first_row + (half * 4 + b) * words, 16)
                a_ref[pl.ds(start, words), cols] = v.astype(jnp.float32).astype(jnp.bfloat16)
        dacc[col] = total
        return carry

    lax.fori_loop(0, blocks * blocks, expand, 0)
    per = block // LANES
    for col in range(blocks):
        sums = jnp.sum(dacc[col], axis=0, keepdims=True).astype(jnp.float32)
        for i in range(per):
            deg_ref[col * per + i:col * per + i + 1, :] = sums[:, i * LANES:(i + 1) * LANES]


def rank_kernel(
    sizes, a_hbm, deg_ref, dang_ref, order_ref, seeds_ref, rank_ref, change_ref,
    a_ref, pos, hist, hist_bf, src_ref, tele_bf, own_bf,
    degs, wcol, dcol, scaled, nat, own_flow, sbuf1, sbuf2, recv_b, recv_c, recv_t,
    rank1, recv_d, lost1, lost2, chg, chg_all, stage, a_sem,
    deg_s, deg_r, h_s, h_r, o_s, o_r, l1_s, l1_r, l2_s, l2_r, b_s, b_r, c_s, c_r, t_s, t_r,
    d_s, d_r, e_s, e_r, f_s, f_r, s_s, s_r,
):
    n_row, n_col, range_hosts, piece, block, host_total, seed_scale = sizes
    words = block // 8
    r = lax.axis_index("row")
    c = lax.axis_index("col")
    total_mass = host_total / 16.0
    chunks = range_hosts // LANES

    def each(n, body):
        lax.fori_loop(0, n, lambda i, carry: (body(i), carry)[1], 0)

    def others(n, mine, body):
        def step(i):
            @pl.when(i != mine)
            def _():
                body(i)
        each(n, step)

    def remote(src, dst, send, recv, row, col):
        return pltpu.make_async_remote_copy(
            src_ref=src, dst_ref=dst, send_sem=send, recv_sem=recv,
            device_id={"row": row, "col": col}, device_id_type=MESH)

    barrier = pltpu.get_barrier_semaphore()
    diagonal = r == c

    def greet(row, col):
        pl.semaphore_signal(barrier, inc=1, device_id={"row": row, "col": col},
                            device_id_type=MESH)

    others(n_row, r, lambda i: greet(i, c))
    others(n_col, c, lambda i: greet(r, i))

    @pl.when(jnp.logical_not(diagonal))
    def _():
        greet(c, r)


    fetch = pltpu.make_async_copy(a_hbm, a_ref, a_sem)
    fetch.start()
    topics, seeds = seeds_ref.shape
    share = topics // n_row
    table_rows = order_ref.shape[0]
    parts = seeds // LANES

    def place(group, carry):
        rows8 = pl.ds(pl.multiple_of(r * share + group * 8, 8), 8)
        ids = [seeds_ref[rows8, h * LANES:(h + 1) * LANES] for h in range(parts)]
        low = [x & (LANES - 1) for x in ids]
        high = [x >> 7 for x in ids]

        def look(t, found):
            row = jnp.broadcast_to(order_ref[pl.ds(t, 1), :], (8, LANES))
            return tuple(
                jnp.where(high[h] == t,
                          jnp.take_along_axis(row, low[h], axis=1, mode="promise_in_bounds"),
                          found[h])
                for h in range(parts)
            )

        found = lax.fori_loop(0, table_rows, look,
                              tuple(jnp.zeros((8, LANES), jnp.int32) for _ in range(parts)),
                              unroll=8)
        for h in range(parts):
            pos[pl.ds(pl.multiple_of(group * 8, 8), 8), h * LANES:(h + 1) * LANES] = found[h]
        return carry

    lax.fori_loop(0, share // 8, place, 0)
    wanted = c * chunks + lax.broadcasted_iota(jnp.int32, (chunks, seeds), 0)
    lane_id = lax.broadcasted_iota(jnp.int32, (LANES, seeds), 0)

    def count(k, carry):
        row = pos[pl.ds(k, 1), :]
        low = jnp.where((row & (LANES - 1)) == lane_id, 1.0, 0.0).astype(jnp.bfloat16)
        high = jnp.where((row >> 7) == wanted, 1.0, 0.0).astype(jnp.bfloat16)
        hist[pl.ds(pl.multiple_of(k * chunks, 8), chunks), :] = lax.dot_general(
            high, low, (((1,), (1,)), ((), ())), preferred_element_type=jnp.float32)
        return carry

    lax.fori_loop(0, share, count, 0, unroll=8)
    hist_bf[r] = hist[pl.ds(0, share * chunks), :].astype(jnp.bfloat16)
    pl.semaphore_wait(barrier, n_row + n_col - 2 + jnp.where(diagonal, 0, 1))

    def deg_copy(i, slot):
        return remote(deg_ref, degs.at[slot], deg_s.at[i], deg_r.at[slot], i, c)

    def hist_copy(i, slot):
        return remote(hist_bf.at[r], hist_bf.at[slot], h_s.at[i], h_r.at[slot], i, c)

    others(n_row, r, lambda i: deg_copy(i, r).start())
    others(n_row, r, lambda i: hist_copy(i, r).start())
    degs[r] = deg_ref[...]
    others(n_row, r, lambda i: deg_copy(i, i).wait_recv())
    degree = degs[0]
    for i in range(1, n_row):
        degree = degree + degs[i]
    weight = ((1.0 - dang_ref[...].astype(jnp.float32)) / jnp.maximum(degree, 1.0)).T
    degree = degree.T
    for i in range(chunks):
        rows = slice(i * LANES, (i + 1) * LANES)
        wcol[rows, :] = jnp.broadcast_to(weight[:, i:i + 1], (LANES, LANES))
        dcol[rows, :] = jnp.broadcast_to(degree[:, i:i + 1], (LANES, LANES))

    others(n_row, r, lambda i: hist_copy(i, i).wait_recv())
    slab = share * chunks
    for i in range(n_row):
        hist[i * slab:(i + 1) * slab, :] = hist_bf[i].astype(jnp.float32)
    for i in range(chunks):
        tele_bf[i * LANES:(i + 1) * LANES, :] = (
            hist[pl.ds(i, topics, stride=chunks), :].T.astype(jnp.bfloat16))
    src_ref[...] = tele_bf[...].astype(jnp.float32) * seed_scale
    quarter = pl.ds(pl.multiple_of(r * piece, piece), piece)
    o_copy = remote(tele_bf.at[quarter], own_bf, o_s, o_r, c, r)

    def make_scaled(source_of, lost, send, recv):
        def step(i, total):
            rows = pl.ds(pl.multiple_of(i * LANES, LANES), LANES)
            part = (source_of(i, rows).astype(jnp.float32) * wcol[rows, :]).astype(jnp.bfloat16)
            scaled[rows, :] = part
            mass = dcol[rows, :] * part.astype(jnp.float32)
            return total + jnp.sum(mass.reshape(LANES // 8, 8, LANES), axis=0)

        lost[c] = lax.fori_loop(0, chunks, step, jnp.zeros((8, LANES), jnp.float32))
        others(n_col, c, lambda i: lost_copy(lost, send, recv, i, c).start())

    def lost_copy(lost, send, recv, i, slot):
        return remote(lost.at[c], lost.at[slot], send.at[i], recv.at[slot], r, i)

    def coefficient(lost, send, recv):
        others(n_col, c, lambda i: lost_copy(lost, send, recv, i, i).wait_recv())
        total = lost[0]
        for i in range(1, n_col):
            total = total + lost[i]
        gone = total_mass - jnp.sum(total, axis=0, keepdims=True)
        return 0.85 * gone / total_mass + 0.15

    def flow_piece(q, sbuf):
        for sub in range(piece // block):
            first = pl.multiple_of(q * piece + sub * block, block)
            product = jnp.dot(a_ref[pl.ds(first, block), :], scaled[...],
                              preferred_element_type=jnp.float32)
            for bit in range(8):
                nat[pl.ds(sub * block + bit, words, stride=8), :] = (
                    product[bit * words:(bit + 1) * words, :])
        sbuf[q] = nat[...].astype(jnp.bfloat16)

    make_scaled(lambda i, rows: src_ref[rows, :].astype(jnp.bfloat16), lost1, l1_s, l1_r)
    fetch.wait()

    def s_copy(q, slot):
        return remote(sbuf1.at[q], stage.at[slot], s_s.at[q], s_r.at[slot], q, c)

    def b_copy(i, slot):
        return remote(stage.at[i], recv_b.at[slot], b_s.at[i], b_r.at[slot], r, i)

    def first_piece(i):
        q = lax.rem(r + 1 + i, n_row)
        flow_piece(q, sbuf1)

        @pl.when(q != r)
        def _():
            s_copy(q, r).start()

        @pl.when(q == r)
        def _():
            stage[r] = sbuf1[q]

    each(n_row, first_piece)

    def pass_on(j):
        i = lax.rem(r + n_row - j, n_row)

        @pl.when(i != r)
        def _():
            s_copy(0, i).wait_recv()

        @pl.when(i != c)
        def _():
            b_copy(i, c).start()

    each(n_row, pass_on)
    recv_b[c] = stage[c]
    share1 = coefficient(lost1, l1_s, l1_r)

    others(n_col, c, lambda i: b_copy(0, i).wait_recv())
    flow = recv_b[0].astype(jnp.float32)
    for i in range(1, n_col):
        flow = flow + recv_b[i].astype(jnp.float32)
    tele = src_ref[quarter, :]
    new_rank = 0.85 * flow + share1 * tele
    recv_c[r] = new_rank.astype(jnp.bfloat16)

    def c_copy(i, slot):
        return remote(recv_c.at[r], recv_c.at[slot], c_s.at[i], c_r.at[slot], i, c)

    others(n_row, r, lambda i: c_copy(i, r).start())
    rank1[...] = new_rank
    t_copy = remote(rank1, recv_t, t_s, t_r, c, r)

    @pl.when(jnp.logical_not(diagonal))
    def _():
        t_copy.start()
        o_copy.start()

    @pl.when(diagonal)
    def _():
        recv_t[...] = rank1[...]
        own_bf[...] = tele_bf[quarter, :]

    others(n_row, r, lambda i: c_copy(i, i).wait_recv())

    per = piece // LANES

    def second_source(i, rows):
        inner = pl.ds(pl.multiple_of((i % per) * LANES, LANES), LANES)
        return recv_c[i // per, inner, :]

    make_scaled(second_source, lost2, l2_s, l2_r)

    def d_copy(q, slot):
        return remote(sbuf2.at[q], recv_d.at[slot], d_s.at[q], d_r.at[slot], r, q)

    def second_piece(i):
        q = lax.rem(c + 1 + i, n_col)
        flow_piece(q, sbuf2)

        @pl.when(q != c)
        def _():
            d_copy(q, c).start()

        @pl.when(q == c)
        def _():
            own_flow[...] = nat[...]

    each(n_col, second_piece)
    share2 = coefficient(lost2, l2_s, l2_r)
    recv_d[c] = jnp.zeros((piece, LANES), jnp.bfloat16)

    @pl.when(jnp.logical_not(diagonal))
    def _():
        t_copy.wait_recv()
        o_copy.wait_recv()

    others(n_col, c, lambda i: d_copy(0, i).wait_recv())
    flow = own_flow[...]
    for i in range(n_col):
        flow = flow + recv_d[i].astype(jnp.float32)
    last = 0.85 * flow + share2 * (own_bf[...].astype(jnp.float32) * seed_scale)
    moved = jnp.abs(last - recv_t[...])
    chg[c] = jnp.sum(moved.reshape(piece // 8, 8, LANES), axis=0)

    def e_copy(i, slot):
        return remote(chg.at[c], chg.at[slot], e_s.at[i], e_r.at[slot], r, i)

    def f_copy(i, slot):
        return remote(chg_all.at[r], chg_all.at[slot], f_s.at[i], f_r.at[slot], i, c)

    others(n_col, c, lambda i: e_copy(i, c).start())
    rank_ref[...] = last
    others(n_col, c, lambda i: e_copy(i, i).wait_recv())
    total = chg[0]
    for i in range(1, n_col):
        total = total + chg[i]
    chg_all[r] = total
    others(n_row, r, lambda i: f_copy(i, r).start())
    others(n_row, r, lambda i: deg_copy(i, r).wait_send())
    others(n_row, r, lambda i: hist_copy(i, r).wait_send())
    others(n_col, c, lambda i: lost_copy(lost1, l1_s, l1_r, i, c).wait_send())
    others(n_col, c, lambda i: lost_copy(lost2, l2_s, l2_r, i, c).wait_send())

    others(n_row, r, lambda i: s_copy(i, r).wait_send())
    others(n_col, c, lambda i: b_copy(i, c).wait_send())
    others(n_row, r, lambda i: c_copy(i, r).wait_send())

    @pl.when(jnp.logical_not(diagonal))
    def _():
        t_copy.wait_send()
        o_copy.wait_send()

    others(n_col, c, lambda i: d_copy(i, c).wait_send())
    others(n_col, c, lambda i: e_copy(i, c).wait_send())
    others(n_row, r, lambda i: f_copy(i, i).wait_recv())
    total = chg_all[0]
    for i in range(1, n_row):
        total = total + chg_all[i]
    change_ref[...] = total
    others(n_row, r, lambda i: f_copy(i, r).wait_send())


def give_kernel(host_total, last_ref, moved_ref, rank_ref, change_ref):
    rank_ref[...] = last_ref[...]
    change_ref[...] = jnp.sum(moved_ref[...], axis=0, keepdims=True) / host_total


def shards(n_row, n_col, tile_bits, tile_rows, tile_cols, tile_count, host_order, seed_hosts,
           dangling):
    packed = tile_bits[0, 0]
    slots, words, block = packed.shape
    host_total = host_order.shape[0]
    range_hosts = dangling.shape[0]
    blocks = range_hosts // block
    topics, seeds = seed_hosts.shape
    piece = range_hosts // n_col
    assert slots < 128 and topics == LANES and n_row == n_col and piece % block == 0
    assert seeds <= 256 and topics % (8 * n_row) == 0
    seed_scale = host_total / (16.0 * seeds)
    f32, bf16, i32 = jnp.float32, jnp.bfloat16, jnp.int32
    chunks = range_hosts // LANES
    vmem = pl.BlockSpec(memory_space=pltpu.VMEM)
    smem = pl.BlockSpec(memory_space=pltpu.SMEM)
    hbm = pl.BlockSpec(memory_space=pl.ANY)
    adjacency, degree = pl.pallas_call(
        functools.partial(cell_kernel, (block, blocks)),
        out_shape=[
            jax.ShapeDtypeStruct((range_hosts, range_hosts), bf16),
            jax.ShapeDtypeStruct((chunks, LANES), f32),
        ],
        in_specs=[smem, smem, smem, hbm],
        out_specs=[vmem] * 2,
        scratch_shapes=[
            pltpu.VMEM((slots, words, block), i32),
            pltpu.VMEM((blocks * blocks, 2, words, block), i32),
            pltpu.VMEM((blocks, words, block), i32),
            pltpu.SemaphoreType.DMA,
        ],
        compiler_params=pltpu.CompilerParams(vmem_limit_bytes=60 * 2**20),
        name="cell",
    )(tile_rows[0, 0], tile_cols[0, 0], tile_count[0], packed)

    dma = lambda n: pltpu.SemaphoreType.DMA((n,))
    last, moved = pl.pallas_call(
        functools.partial(rank_kernel, (n_row, n_col, range_hosts, piece, block, host_total,
                                        seed_scale)),
        out_shape=[
            jax.ShapeDtypeStruct((piece, topics), f32),
            jax.ShapeDtypeStruct((8, topics), f32),
        ],
        in_specs=[hbm] + [vmem] * 4,
        out_specs=[vmem] * 2,
        scratch_shapes=[
            pltpu.VMEM((range_hosts, range_hosts), bf16),
            pltpu.VMEM((topics // n_row, seeds), i32),
            pltpu.VMEM((topics * chunks, LANES), f32),
            pltpu.VMEM((n_row, topics // n_row * chunks, LANES), bf16),
            pltpu.VMEM((range_hosts, topics), f32),
            pltpu.VMEM((range_hosts, topics), bf16),
            pltpu.VMEM((piece, topics), bf16),
            pltpu.VMEM((n_row, chunks, LANES), f32),
            pltpu.VMEM((range_hosts, topics), f32),
            pltpu.VMEM((range_hosts, topics), f32),
            pltpu.VMEM((range_hosts, topics), bf16),
            pltpu.VMEM((piece, topics), f32),
            pltpu.VMEM((piece, topics), f32),
            pltpu.VMEM((n_row, piece, topics), bf16),
            pltpu.VMEM((n_col, piece, topics), bf16),
            pltpu.VMEM((n_col, piece, topics), bf16),
            pltpu.VMEM((n_row, piece, topics), bf16),
            pltpu.VMEM((piece, topics), f32),
            pltpu.VMEM((piece, topics), f32),
            pltpu.VMEM((n_col, piece, topics), bf16),
            pltpu.VMEM((n_col, 8, topics), f32),
            pltpu.VMEM((n_col, 8, topics), f32),
            pltpu.VMEM((n_col, 8, topics), f32),
            pltpu.VMEM((n_row, 8, topics), f32),
            pltpu.VMEM((n_row, piece, topics), bf16),
            pltpu.SemaphoreType.DMA,
            dma(n_row), dma(n_row), dma(n_row), dma(n_row),
            pltpu.SemaphoreType.DMA, pltpu.SemaphoreType.DMA,
            dma(n_col), dma(n_col), dma(n_col), dma(n_col),
            dma(n_row), dma(n_col),
            dma(n_row), dma(n_row),
            pltpu.SemaphoreType.DMA, pltpu.SemaphoreType.DMA,
            dma(n_col), dma(n_col),
            dma(n_col), dma(n_col), dma(n_row), dma(n_row), dma(n_row), dma(n_row),
        ],
        compiler_params=pltpu.CompilerParams(
            collective_id=0, has_side_effects=True, vmem_limit_bytes=60 * 2**20),
        name="iterate",
    )(adjacency, degree, dangling.reshape(chunks, LANES),
      host_order.reshape(host_total // LANES, LANES), seed_hosts)
    rank, change = pl.pallas_call(
        functools.partial(give_kernel, host_total),
        out_shape=[
            jax.ShapeDtypeStruct((piece, topics), f32),
            jax.ShapeDtypeStruct((1, topics), f32),
        ],
        in_specs=[vmem] * 2,
        out_specs=[vmem] * 2,
        name="give",
    )(last, moved)
    return (rank, change.reshape(topics))


def solution(mesh):
    in_specs = (
        P(("groups", "row"), "col", None, None, None),
        P(("groups", "row"), "col", None),
        P(("groups", "row"), "col", None),
        P(("groups", "row"), "col"),
        P("groups"),
        P("groups", None),
        P(("groups", "col")),
    )
    out_specs = (P(("groups", "row", "col"), None), P("groups"))
    body = functools.partial(shards, mesh.shape["row"], mesh.shape["col"])
    return jax.shard_map(body, mesh=mesh, in_specs=in_specs, out_specs=out_specs, check_vma=False)
```
